256 devices in a mesh: grp: 4 (over y), row: 16 (over z, core), col: 4 (over x).
Axes of the slice: x: 4, y: 4, z: 8, core: 2. Of those that a mesh axis runs over, the one named last changes fastest.
Arguments:
- matrix: float32 [32768, 8192], P(('grp', 'row'), 'col'), parts along dimension 0, as said below
- basis_matrix: float32 [32768, 8192], P(('grp', 'row'), 'col'), parts along dimension 0, as said below
- panel_index: int32 [8, 2], P('grp'), parts along dimension 0, may hold values from 0 to 31, as said below
Outputs:
- projected: float32 [32768, 256], P(('grp', 'col', 'row')), parts along dimension 0
The draws below stay inside these ranges and needn't reach their ends.
There are 4 independent parts, one for each index of `grp`. The reference program is written for one: setup_inputs(seed, part) draws one part's arguments, and reference() takes and returns one part's arrays. A program takes and returns all parts, laid end to end along the dimension named above; each array names one. Nothing has to cross between parts.
Inputs may be any that keep to these rules, and one draw needn't show every extreme that they name: matrix is symmetric. The columns of basis_matrix are orthonormal. `panel_index`: row h names panels of half h; some half names panel 0 and some names the last panel.
All inputs are finite; a program needn't handle non-finite values.
Results may differ from the reference program's by a relative error of at most 0.00007.
Values sent between devices are 32-bit elements; how exact they have to be, the bound alone decides.
A program may use at most 64 MiB of HBM per device.

```python
import math
import jax
import jax.numpy as jnp
from jax import lax

ORDER = 8192
PANEL = 128
PANELS = 2


def parity_sign(row_ids, col_ids):
    common = jnp.bitwise_and(row_ids, col_ids)
    parity = jnp.zeros(common.shape, jnp.int32)
    for bit_number in range(ORDER.bit_length()):
        parity = jnp.bitwise_xor(parity, jnp.bitwise_and(jnp.right_shift(common, bit_number), 1))
    return (1 - 2 * parity).astype(jnp.float32)


def draw_matrix(key, part):
    key = jax.random.fold_in(key, 11)
    normal_key = jax.random.fold_in(key, 0)
    entries = jax.random.normal(normal_key, (ORDER, ORDER), jnp.float32)
    symmetric = (entries + entries.T) * 0.7071
    return symmetric


def draw_basis_matrix(key, part):
    key = jax.random.fold_in(key, 23)
    perm_key, theta_key, phi_key, section_key = jax.random.split(key, 4)
    shuffle = jax.random.permutation(perm_key, ORDER).astype(jnp.int32)
    theta = jax.random.uniform(theta_key, (ORDER // 2,), jnp.float32, -math.pi, math.pi)
    angles = jax.random.uniform(phi_key, (ORDER // 2,), jnp.float32, -math.pi, math.pi)
    row_ids = jnp.arange(ORDER, dtype=jnp.int32)[:, None]
    col_ids = jnp.arange(ORDER, dtype=jnp.int32)[None, :]
    pair_col = col_ids // 2
    first_col = shuffle[pair_col * 2]
    second_col = shuffle[pair_col * 2 + 1]
    cos_col = jnp.cos(theta)[pair_col]
    sin_col = jnp.sin(theta)[pair_col]
    odd_col = col_ids % 2 == 1

    def column_mix(rows_used):
        sign_first = parity_sign(rows_used, first_col)
        sign_second = parity_sign(rows_used, second_col)
        return jnp.where(odd_col, sin_col * sign_first + cos_col * sign_second, cos_col * sign_first - sin_col * sign_second)
    pair_row = row_ids // 2
    even_rows = column_mix(pair_row * 2)
    odd_rows = column_mix(pair_row * 2 + 1)
    cos_row = jnp.cos(angles)[pair_row]
    sin_row = jnp.sin(angles)[pair_row]
    odd_row = row_ids % 2 == 1
    mixed = jnp.where(odd_row, sin_row * even_rows + cos_row * odd_rows, cos_row * even_rows - sin_row * odd_rows)
    flat_rows = jnp.arange(ORDER, dtype=jnp.int32)
    bit_number = 1
    while 1 << bit_number < ORDER:
        stride = 1 << bit_number
        section_angles = jax.random.uniform(jax.random.fold_in(section_key, bit_number), (ORDER,), jnp.float32, -math.pi, math.pi)
        partner_rows = jnp.bitwise_xor(flat_rows, stride)
        lower_rows = jnp.minimum(flat_rows, partner_rows)
        section_cos = jnp.cos(section_angles)[lower_rows][:, None]
        section_sin = jnp.sin(section_angles)[lower_rows][:, None]
        upper_member = (jnp.bitwise_and(flat_rows, stride) != 0)[:, None]
        partner_values = mixed[partner_rows]
        mixed = jnp.where(upper_member, section_sin * partner_values + section_cos * mixed, section_cos * mixed - section_sin * partner_values)
        bit_number = bit_number + 1
    return mixed / math.sqrt(ORDER)


def draw_panel_index(key, part):
    key = jax.random.fold_in(key, 37)
    first_key, second_key, half_key, slot_key = jax.random.split(key, 4)
    count = ORDER // 2 // PANEL
    first_half = jax.random.permutation(first_key, count)[:PANELS]
    second_half = jax.random.permutation(second_key, count)[:PANELS]
    table = jnp.stack([first_half, second_half]).astype(jnp.int32)
    which_half = jax.random.randint(half_key, (), 0, 2)
    which_slot = jax.random.randint(slot_key, (), 0, PANELS)
    table = table.at[which_half, which_slot].set(count - 1)
    table = table.at[1 - which_half, which_slot].set(0)
    return table


def setup_inputs(seed: int = 0, part: int = 0) -> dict:
    key_of = jax.random.split(jax.random.key(seed), 4)
    part_keys = jax.random.split(jax.random.fold_in(key_of[3], part), 4)
    matrix = draw_matrix(jax.random.fold_in(jax.random.fold_in(key_of[3], part), 71), part)
    basis_matrix = draw_basis_matrix(jax.random.fold_in(jax.random.fold_in(key_of[3], part), 71), part)
    panel_index = draw_panel_index(jax.random.fold_in(jax.random.fold_in(key_of[3], part), 71), part)
    return {"matrix": matrix, "basis_matrix": basis_matrix, "panel_index": panel_index}


def reference(matrix, basis_matrix, panel_index):
    half_order = ORDER // 2
    panel_width = PANELS * PANEL
    offsets = jnp.arange(PANEL, dtype=jnp.int32)
    starts = panel_index.astype(jnp.int32) * PANEL + (jnp.arange(2, dtype=jnp.int32) * half_order)[:, None]
    indices = (starts[:, :, None] + offsets[None, None, :]).reshape(-1).astype(jnp.int32)
    chosen = jnp.take(basis_matrix, indices, axis=1)
    images = jnp.dot(matrix, chosen, precision=lax.Precision.HIGHEST, preferred_element_type=jnp.float32)
    upper = jnp.dot(basis_matrix[:, :half_order].T, images[:, :panel_width], precision=lax.Precision.HIGHEST, preferred_element_type=jnp.float32)
    lower_part = jnp.dot(basis_matrix[:, half_order:].T, images[:, panel_width:], precision=lax.Precision.HIGHEST, preferred_element_type=jnp.float32)
    return jnp.concatenate([upper, lower_part], axis=0)
```

```python
import functools

import jax
import jax.numpy as jnp
from jax import lax
from jax.experimental import pallas as pl
from jax.experimental.pallas import tpu as pltpu
from jax.sharding import PartitionSpec as P

PANEL = 128
MESH = pl.DeviceIdType.MESH
PLANES = 8
COLS = 4
UNITS = 2
BF16 = jnp.bfloat16
F32 = jnp.float32


def split(value):
    high = value.astype(BF16)
    return high, (value - high.astype(F32)).astype(BF16)


def dot3(a_high, a_low, b_high, b_low):
    total = jnp.dot(a_high, b_high, preferred_element_type=F32)
    total += jnp.dot(a_high, b_low, preferred_element_type=F32)
    total += jnp.dot(a_low, b_high, preferred_element_type=F32)
    return total


def kernel(
    index_ref, matrix_hbm, basis_hbm, out_ref,
    matrix_v, basis_v, m_high, m_low, qt_high, qt_low,
    pair_out, pair_in, ring, chosen, x_high, x_low,
    image, image_in, image_sum, image_pair,
    proj, proj_in, proj_sum, up_out, up_in, down_out, down_in,
    load_sem, pair_s, pair_r, up_s, up_r, down_s, down_r,
    cross_s, cross_r, twin_s, twin_r, swap_s, swap_r, half_s, half_r,
    mate_s, mate_r, sum_up_s, sum_up_r, sum_down_s, sum_down_r,
):
    grp = lax.axis_index("grp")
    row = lax.axis_index("row")
    col = lax.axis_index("col")
    plane = row // 2
    core = lax.rem(row, 2)
    half = col // 2
    slot = lax.rem(col, 2)
    rows = basis_v.shape[0]
    cols = basis_v.shape[1]
    unit = rows // UNITS
    piece = cols // (2 * PLANES)
    per_col = cols // PANEL

    def at(r, c):
        return (grp, r, c)

    twin = at(row + 1 - 2 * core, col)
    above = at(lax.rem(plane + 1, PLANES) * 2 + core, col)
    below = at(lax.rem(plane + PLANES - 1, PLANES) * 2 + core, col)
    pair = at(row, col + 1 - 2 * slot)
    mirror = at(row, 3 - col)
    across = at(row, lax.rem(col + 2, COLS))

    load_basis = pltpu.make_async_copy(basis_hbm, basis_v, load_sem.at[0])
    load_matrix = pltpu.make_async_copy(matrix_hbm, matrix_v, load_sem.at[1])
    load_basis.start()
    load_matrix.start()

    barrier = pltpu.get_barrier_semaphore()
    for other in (twin, above, below, pair, mirror, across):
        pl.semaphore_signal(barrier, inc=1, device_id=other, device_id_type=MESH)
    pl.semaphore_wait(barrier, 6)

    sends = []

    def send(src, dst, send_sem, recv_sem, target):
        copy = pltpu.make_async_remote_copy(
            src_ref=src, dst_ref=dst, send_sem=send_sem, recv_sem=recv_sem,
            device_id=target, device_id_type=MESH,
        )
        copy.start()
        sends.append(copy)

    def arrived(ref, sem):
        pltpu.make_async_copy(ref, ref, sem).wait()

    def part(u):
        return pl.ds(u * unit, unit)

    load_basis.wait()

    own = index_ref[half, slot] - slot * per_col
    other = index_ref[half, 1 - slot] - slot * per_col
    span_rows = min(64, rows)

    def pick(i, carry):
        at_rows = pl.ds(pl.multiple_of(i * span_rows, span_rows), span_rows)
        own_v = jnp.full((span_rows, PANEL), own, jnp.int32)
        other_v = jnp.full((span_rows, PANEL), other, jnp.int32)
        own_value = jnp.zeros((span_rows, PANEL), F32)
        other_value = own_value
        for j in range(per_col):
            value = basis_v[at_rows, j * PANEL:(j + 1) * PANEL]
            own_value = jnp.where(own_v == j, value, own_value)
            other_value = jnp.where(other_v == j, value, other_value)
        ring[0, at_rows] = own_value
        pair_out[at_rows] = other_value
        return carry

    lax.fori_loop(0, rows // span_rows, pick, 0)
    for u in range(UNITS):
        send(pair_out.at[part(u)], pair_in.at[part(u)], pair_s.at[u], pair_r.at[u], pair)

    def split_matrix(b):
        at_cols = pl.ds(b * rows, rows)
        high, low = split(matrix_v[:, at_cols])
        m_high[:, at_cols] = high
        m_low[:, at_cols] = low

    def split_basis(b):
        def body(i, carry):
            at_cols = pl.ds(pl.multiple_of(b * rows + i * PANEL, PANEL), PANEL)
            high, low = split(basis_v[:, at_cols].T)
            qt_high[at_cols, :] = high
            qt_low[at_cols, :] = low
            return carry
        lax.fori_loop(0, rows // PANEL, body, 0)

    cross = []

    def deliver(d, u):
        source = lax.rem(plane + PLANES - d, PLANES)
        target = source // 2
        odd = lax.rem(source, 2)
        src = ring.at[d, part(u)]
        dst = chosen.at[2 * odd + core, col, part(u)]
        sem = cross_r.at[odd, col, u]
        copy = pltpu.make_async_remote_copy(
            src_ref=src, dst_ref=dst, send_sem=cross_s.at[d, u], recv_sem=sem,
            device_id=at(row, target), device_id_type=MESH,
        )

        @pl.when(target != col)
        def _():
            copy.start()

        @pl.when(target == col)
        def _():
            pltpu.make_async_copy(src, dst, sem).start()

        cross.append((target, copy))

    def go_up(d, u):
        send(ring.at[d, part(u)], ring.at[d + 1, part(u)], up_s.at[d, u], up_r.at[d, u], above)

    def go_down(d, u):
        send(
            ring.at[(PLANES - d) % PLANES, part(u)], ring.at[PLANES - 1 - d, part(u)],
            down_s.at[d, u], down_r.at[d, u], below,
        )

    for u in range(UNITS):
        arrived(pair_in.at[part(u)], pair_r.at[u])
        ring[0, part(u)] = ring[0, part(u)] + pair_in[part(u)]
        go_up(0, u)
        go_down(0, u)
        deliver(0, u)
    load_matrix.wait()
    work = [functools.partial(split_matrix, b) for b in range(4)]
    work += [functools.partial(split_basis, b) for b in range(4)]
    for d in range(1, 5):
        for u in range(UNITS):
            if work:
                work.pop(0)()
            if d < 4 or u == 0:
                arrived(ring.at[d, part(u)], up_r.at[d - 1, u])
                if d < 3 or (d == 3 and u == 0):
                    go_up(d, u)
            if d < 4 or u == 1:
                arrived(ring.at[PLANES - d, part(u)], down_r.at[d - 1, u])
                if d < 3 or (d == 3 and u == 1):
                    go_down(d, u)
            deliver(d, u)
            if d < 4:
                deliver(PLANES - d, u)

    def prepare(block):
        for h in range(2):
            value = jnp.concatenate([chosen[block, 2 * h], chosen[block, 2 * h + 1]], axis=1)
            x_high[h], x_low[h] = split(value)

    step = 256 if rows % 256 == 0 else rows

    def multiply(block, h, first):
        at_cols = pl.ds(pl.multiple_of(block * rows, rows), rows)

        def body(i, carry):
            at_rows = pl.ds(pl.multiple_of(i * step, step), step)
            value = dot3(m_high[at_rows, at_cols], m_low[at_rows, at_cols], x_high[h], x_low[h])
            for q in range(2):
                term = value[:, q * PANEL:(q + 1) * PANEL]
                image[2 * h + q, at_rows] = term if first else image[2 * h + q, at_rows] + term
            return carry
        lax.fori_loop(0, rows // step, body, 0)

    for odd in range(2):
        for p in range(COLS):
            for u in range(UNITS):
                ref = chosen.at[2 * odd + core, p, part(u)]
                arrived(ref, cross_r.at[odd, p, u])
                send(ref, ref, twin_s.at[odd, p, u], twin_r.at[odd, p, u], twin)
        prepare(2 * odd + core)
        multiply(2 * odd + core, 0, odd == 0)
        multiply(2 * odd + core, 1, odd == 0)
    for odd in range(2):
        for p in range(COLS):
            for u in range(UNITS):
                arrived(chosen.at[2 * odd + 1 - core, p, part(u)], twin_r.at[odd, p, u])
        prepare(2 * odd + 1 - core)
        multiply(2 * odd + 1 - core, 1 - half, False)
        if odd == 1:
            for q in range(2):
                for u in range(UNITS):
                    send(
                        image.at[2 * (1 - half) + q, part(u)], image_in.at[q, part(u)],
                        swap_s.at[q, u], swap_r.at[q, u], mirror,
                    )
        multiply(2 * odd + 1 - core, half, False)

    for q in range(2):
        for u in range(UNITS):
            arrived(image_in.at[q, part(u)], swap_r.at[q, u])
            image_sum[q, part(u)] = image[2 * half + q, part(u)] + image_in[q, part(u)]
            send(
                image_sum.at[q, part(u)], image_pair.at[q, part(u)],
                half_s.at[q, u], half_r.at[q, u], pair,
            )

    def project(q, parity):
        def body(i, carry):
            at_rows = pl.ds(pl.multiple_of((2 * i + parity) * piece, piece), piece)
            proj[q, parity, i] = dot3(
                qt_high[at_rows, :], qt_low[at_rows, :],
                x_high[q, :, :PANEL], x_low[q, :, :PANEL],
            )
            return carry
        lax.fori_loop(0, PLANES, body, 0)

    near = piece // 2

    def span(d, up):
        if d < 4:
            return pl.ds(0, piece)
        return pl.ds(0, near) if up else pl.ds(near, near)

    def sum_step(q, d):
        for up in (True, False):
            buf_out, buf_in = (up_out, up_in) if up else (down_out, down_in)
            s_sem, r_sem = (sum_up_s, sum_up_r) if up else (sum_down_s, sum_down_r)
            target = lax.rem(plane + (d if up else PLANES - d), PLANES)
            here = span(d, up)
            if d < 4:
                got = span(d + 1, up)
                arrived(buf_in.at[q, d, got], r_sem.at[q, d])
                buf_out[q, d, here] = proj_sum[q, target]
                buf_out[q, d, got] = buf_out[q, d, got] + buf_in[q, d, got]
            else:
                buf_out[q, d, here] = proj_sum[q, target, here]
            send(
                buf_out.at[q, d, here], buf_in.at[q, d - 1, here],
                s_sem.at[q, d], r_sem.at[q, d - 1], above if up else below,
            )

    def begin(q):
        for u in range(UNITS):
            arrived(image_pair.at[q, part(u)], half_r.at[q, u])
        high, low = split(image_sum[q] + image_pair[q])
        x_high[q, :, :PANEL] = high
        x_low[q, :, :PANEL] = low
        project(q, 1 - core)
        send(proj.at[q, 1 - core], proj_in.at[q], mate_s.at[q], mate_r.at[q], twin)
        project(q, core)

    def combine(q):
        arrived(proj_in.at[q], mate_r.at[q])
        proj_sum[q] = proj[q, core] + proj_in[q]

    def finish(q):
        arrived(up_in.at[q, 0], sum_up_r.at[q, 0])
        arrived(down_in.at[q, 0], sum_down_r.at[q, 0])
        out_ref[:, q * PANEL:(q + 1) * PANEL] = proj_sum[q, plane] + up_in[q, 0] + down_in[q, 0]

    begin(0)
    combine(0)
    sum_step(0, 4)
    begin(1)
    sum_step(0, 3)
    combine(1)
    sum_step(1, 4)
    sum_step(0, 2)
    sum_step(1, 3)
    sum_step(0, 1)
    sum_step(1, 2)
    finish(0)
    sum_step(1, 1)
    finish(1)

    for copy in sends:
        copy.wait_send()
    for target, copy in cross:
        @pl.when(target != col)
        def _(copy=copy):
            copy.wait_send()


def body(matrix, basis_matrix, panel_index):
    rows, cols = matrix.shape
    piece = cols // (2 * PLANES)
    vmem = pltpu.VMEM
    dma = pltpu.SemaphoreType.DMA
    return pl.pallas_call(
        kernel,
        out_shape=jax.ShapeDtypeStruct((piece, 2 * PANEL), F32),
        in_specs=[
            pl.BlockSpec(memory_space=pltpu.SMEM),
            pl.BlockSpec(memory_space=pl.ANY),
            pl.BlockSpec(memory_space=pl.ANY),
        ],
        out_specs=pl.BlockSpec(memory_space=pltpu.VMEM),
        scratch_shapes=[
            vmem((rows, cols), F32),
            vmem((rows, cols), F32),
            vmem((rows, cols), BF16),
            vmem((rows, cols), BF16),
            vmem((cols, rows), BF16),
            vmem((cols, rows), BF16),
            vmem((rows, PANEL), F32),
            vmem((rows, PANEL), F32),
            vmem((PLANES, rows, PANEL), F32),
            vmem((4, COLS, rows, PANEL), F32),
            vmem((2, rows, 2 * PANEL), BF16),
            vmem((2, rows, 2 * PANEL), BF16),
            vmem((4, rows, PANEL), F32),
            vmem((2, rows, PANEL), F32),
            vmem((2, rows, PANEL), F32),
            vmem((2, rows, PANEL), F32),
            vmem((2, 2, PLANES, piece, PANEL), F32),
            vmem((2, PLANES, piece, PANEL), F32),
            vmem((2, PLANES, piece, PANEL), F32),
            vmem((2, 5, piece, PANEL), F32),
            vmem((2, 4, piece, PANEL), F32),
            vmem((2, 5, piece, PANEL), F32),
            vmem((2, 4, piece, PANEL), F32),
            dma((2,)),
            dma((UNITS,)), dma((UNITS,)),
            dma((4, UNITS)), dma((4, UNITS)),
            dma((4, UNITS)), dma((4, UNITS)),
            dma((PLANES, UNITS)), dma((2, COLS, UNITS)),
            dma((2, COLS, UNITS)), dma((2, COLS, UNITS)),
            dma((2, UNITS)), dma((2, UNITS)),
            dma((2, UNITS)), dma((2, UNITS)),
            dma((2,)), dma((2,)),
            dma((2, 5)), dma((2, 4)),
            dma((2, 5)), dma((2, 4)),
        ],
        compiler_params=pltpu.CompilerParams(
            collective_id=0, has_side_effects=True, vmem_limit_bytes=56 * 2**20
        ),
        name="project_panels",
    )(panel_index, matrix, basis_matrix)


def solution(mesh):
    return jax.shard_map(
        body,
        mesh=mesh,
        in_specs=(P(("grp", "row"), "col"), P(("grp", "row"), "col"), P("grp", None)),
        out_specs=P(("grp", "col", "row"), None),
        check_vma=False,
    )
```

```python
import functools

import jax
import jax.numpy as jnp
from jax import lax
from jax.experimental import pallas as pl
from jax.experimental.pallas import tpu as pltpu
from jax.sharding import PartitionSpec as P

PANEL = 128
MESH = pl.DeviceIdType.MESH
PLANES = 8
COLS = 4
PASSES = 2
UNITS = 4
PARTS = 2
BF16 = jnp.bfloat16
F32 = jnp.float32


def split(value):
    high = value.astype(BF16)
    return high, (value - high.astype(F32)).astype(BF16)


def dot3(a_high, a_low, b_high, b_low):
    total = jnp.dot(a_high, b_high, preferred_element_type=F32)
    total += jnp.dot(a_high, b_low, preferred_element_type=F32)
    total += jnp.dot(a_low, b_high, preferred_element_type=F32)
    return total


def kernel(
    index_ref, matrix_hbm, basis_hbm, out_ref,
    matrix_v, basis_v, m_high, m_low, qt_high, qt_low,
    pair_out, pair_in, ring, chosen, x_high, x_low, y_high, y_low,
    image, image_in, image_sum, image_pair,
    proj, proj_in, proj_sum, far_in, mid_out, mid_in, near_in,
    load_sem, pair_s, pair_r, up_s, up_r, down_s, down_r,
    cross_s, cross_r, twin_s, twin_r, swap_s, swap_r, half_s, half_r,
    mate_s, mate_r, far_s, far_r, mid_s, mid_r, near_s, near_r,
):
    grp = lax.axis_index("grp")
    row = lax.axis_index("row")
    col = lax.axis_index("col")
    plane = row // 2
    core = lax.rem(row, 2)
    half = col // 2
    slot = lax.rem(col, 2)
    rows = basis_v.shape[0]
    cols = basis_v.shape[1]
    piece = cols // (2 * PLANES)
    per_col = cols // PANEL
    carried = rows // 2
    unit = carried // UNITS
    portion = carried // PARTS

    def at(r, c):
        return (grp, r, c)

    def along(step):
        return at(lax.rem(plane + PLANES + step, PLANES) * 2 + core, col)

    twin = at(row + 1 - 2 * core, col)
    above = along(1)
    below = along(-1)
    pair = at(row, col + 1 - 2 * slot)
    mirror = at(row, 3 - col)
    across = at(row, lax.rem(col + 2, COLS))

    load_basis = pltpu.make_async_copy(basis_hbm, basis_v, load_sem.at[0])
    load_matrix = pltpu.make_async_copy(matrix_hbm, matrix_v, load_sem.at[1])
    load_basis.start()

    barrier = pltpu.get_barrier_semaphore()
    partners = (twin, above, below, along(2), along(-2), pair, mirror, across)
    for other in partners:
        pl.semaphore_signal(barrier, inc=1, device_id=other, device_id_type=MESH)

    sends = []

    def send(src, dst, send_sem, recv_sem, target):
        copy = pltpu.make_async_remote_copy(
            src_ref=src, dst_ref=dst, send_sem=send_sem, recv_sem=recv_sem,
            device_id=target, device_id_type=MESH,
        )
        copy.start()
        sends.append(copy)

    def arrived(ref, sem):
        pltpu.make_async_copy(ref, ref, sem).wait()

    load_basis.wait()
    load_matrix.start()
    span_rows = min(64, carried)

    def pick(s, i, row_half):
        index = index_ref[half, s] - slot * per_col
        at_rows = pl.ds(pl.multiple_of(row_half * carried + i * span_rows, span_rows), span_rows)
        index_v = jnp.full((span_rows, PANEL), index, jnp.int32)
        total = jnp.zeros((span_rows, PANEL), F32)
        for j in range(per_col):
            total = jnp.where(index_v == j, basis_v[at_rows, j * PANEL:(j + 1) * PANEL], total)
        return total

    def pick_other(i, carry):
        for s in range(PASSES):
            at_rows = pl.ds(pl.multiple_of(i * span_rows, span_rows), span_rows)
            pair_out[s, at_rows] = pick(s, i, 1 - slot)
        return carry

    def pick_own(i, carry):
        for s in range(PASSES):
            at_rows = pl.ds(pl.multiple_of(i * span_rows, span_rows), span_rows)
            ring[0, s, at_rows] = pick(s, i, slot)
        return carry

    lax.fori_loop(0, carried // span_rows, pick_other, 0)
    pl.semaphore_wait(barrier, len(partners))

    def of_unit(u):
        return pl.ds(u * unit, unit)

    def of_portion(v):
        return pl.ds(v * portion, portion)

    for s in range(PASSES):
        for u in range(UNITS):
            send(
                pair_out.at[s, of_unit(u)], pair_in.at[s, of_unit(u)],
                pair_s.at[s, u], pair_r.at[s, u], pair,
            )
    lax.fori_loop(0, carried // span_rows, pick_own, 0)

    def split_matrix(b):
        at_cols = pl.ds(b * 2 * PANEL, 2 * PANEL)
        m_high[:, at_cols], m_low[:, at_cols] = split(matrix_v[:, at_cols])

    def split_basis(b):
        at_cols = pl.ds(b * PANEL, PANEL)
        qt_high[at_cols, :], qt_low[at_cols, :] = split(basis_v[:, at_cols].T)

    matrix_work = [functools.partial(split_matrix, b) for b in range(cols // (2 * PANEL))]
    basis_work = [functools.partial(split_basis, b) for b in range(cols // PANEL)]

    def do(work, count):
        for _ in range(min(count, len(work))):
            work.pop(0)()

    cross = []

    def deliver(s, d, v):
        source = lax.rem(plane + PLANES - d, PLANES)
        target = source // 2
        odd = lax.rem(source, 2)
        src = ring.at[d, s, of_portion(v)]
        first = pl.multiple_of(slot * carried + v * portion, portion)
        dst = chosen.at[2 * odd + core, 2 * half + s, pl.ds(first, portion)]
        sem = cross_r.at[odd, s, col, v]
        copy = pltpu.make_async_remote_copy(
            src_ref=src, dst_ref=dst, send_sem=cross_s.at[d, s, v], recv_sem=sem,
            device_id=at(row, target), device_id_type=MESH,
        )

        @pl.when(target != col)
        def _():
            copy.start()

        @pl.when(target == col)
        def _():
            pltpu.make_async_copy(src, dst, sem).start()

        cross.append((target, copy))

    def go_up(s, d, u):
        send(
            ring.at[d, s, of_unit(u)], ring.at[d + 1, s, of_unit(u)],
            up_s.at[d, s, u], up_r.at[d, s, u], above,
        )

    def go_down(s, d, u):
        send(
            ring.at[(PLANES - d) % PLANES, s, of_unit(u)],
            ring.at[PLANES - 1 - d, s, of_unit(u)],
            down_s.at[d, s, u], down_r.at[d, s, u], below,
        )

    def handle(s, d):
        for u in range(UNITS):
            up_far, down_far = u % 2 == 0, u % 2 == 1
            if d == 0:
                arrived(pair_in.at[s, of_unit(u)], pair_r.at[s, u])
                ring[0, s, of_unit(u)] = ring[0, s, of_unit(u)] + pair_in[s, of_unit(u)]
                go_up(s, 0, u)
                go_down(s, 0, u)
            if d > 0 and (d < 4 or up_far):
                arrived(ring.at[d, s, of_unit(u)], up_r.at[d - 1, s, u])
                if d < 3 or (d == 3 and up_far):
                    go_up(s, d, u)
            if d > 0 and (d < 4 or down_far):
                arrived(ring.at[PLANES - d, s, of_unit(u)], down_r.at[d - 1, s, u])
                if d < 3 or (d == 3 and down_far):
                    go_down(s, d, u)
            if u % 2 == 1:
                deliver(s, d, u // 2)
                if 0 < d < 4:
                    deliver(s, PLANES - d, u // 2)

    def share(s, odd):
        for v in range(PARTS):
            for c in range(COLS):
                first = (c % 2) * carried + v * portion
                ref = chosen.at[2 * odd + core, 2 * (c // 2) + s, pl.ds(first, portion)]
                arrived(ref, cross_r.at[odd, s, c, v])
                send(ref, ref, twin_s.at[odd, s, c, v], twin_r.at[odd, s, c, v], twin)

    def shared(s, odd):
        for v in range(PARTS):
            for c in range(COLS):
                first = (c % 2) * carried + v * portion
                ref = chosen.at[2 * odd + 1 - core, 2 * (c // 2) + s, pl.ds(first, portion)]
                arrived(ref, twin_r.at[odd, s, c, v])

    def multiply(s, block, first):
        value = jnp.concatenate([chosen[block, s], chosen[block, 2 + s]], axis=1)
        x_high[...], x_low[...] = split(value)
        at_cols = pl.ds(pl.multiple_of(block * rows, rows), rows)

        def body(i, carry):
            at_rows = pl.ds(pl.multiple_of(i * carried, carried), carried)
            term = dot3(m_high[at_rows, at_cols], m_low[at_rows, at_cols], x_high[...], x_low[...])
            for h in range(2):
                piece_h = term[:, h * PANEL:(h + 1) * PANEL]
                image[s, h, at_rows] = piece_h if first else image[s, h, at_rows] + piece_h
            return carry
        lax.fori_loop(0, 2, body, 0)

    def half_rows(v):
        return pl.ds(v * carried, carried)

    def swap(s, v):
        send(
            image.at[s, 1 - half, half_rows(v)], image_in.at[s, half_rows(v)],
            swap_s.at[s, v], swap_r.at[s, v], mirror,
        )

    def add_swap(s, v):
        at_rows = half_rows(v)
        arrived(image_in.at[s, at_rows], swap_r.at[s, v])
        image_sum[s, at_rows] = image[s, half, at_rows] + image_in[s, at_rows]
        send(
            image_sum.at[s, at_rows], image_pair.at[s, at_rows],
            half_s.at[s, v], half_r.at[s, v], pair,
        )

    order = (4, 3, 5, 2, 6, 1, 7, 0)
    groups = ((0, 3), (3, 8))

    def project(s, parity, group):
        for i in range(*groups[group]):
            target = lax.rem(plane + order[i], PLANES)
            at_rows = pl.ds(pl.multiple_of((2 * target + parity) * piece, piece), piece)
            proj[s, parity, i] = dot3(
                qt_high[at_rows, :], qt_low[at_rows, :], y_high[s], y_low[s]
            )

    def begin(s):
        for v in range(2):
            arrived(image_pair.at[s, half_rows(v)], half_r.at[s, v])
        y_high[s], y_low[s] = split(image_sum[s] + image_pair[s])

    def exchange(s, group):
        first, last = groups[group]
        span_i = pl.ds(first, last - first)
        project(s, 1 - core, group)
        send(
            proj.at[s, 1 - core, span_i], proj_in.at[s, span_i],
            mate_s.at[s, group], mate_r.at[s, group], twin,
        )
        project(s, core, group)

    def combine(s, group):
        first, last = groups[group]
        span_i = pl.ds(first, last - first)
        arrived(proj_in.at[s, span_i], mate_r.at[s, group])
        proj_sum[s, span_i] = proj[s, core, span_i] + proj_in[s, span_i]

    near_rows = piece // 2

    def whole(sign):
        return pl.ds(0, near_rows) if sign == 0 else pl.ds(near_rows, near_rows)

    def place(sign, d):
        return order.index(d if sign == 0 else PLANES - d)

    def toward(sign, d):
        return along(d if sign == 0 else -d)

    def sum_far(s):
        for sign in range(2):
            send(
                proj_sum.at[s, place(sign, 4), whole(sign)], far_in.at[s, sign, 1, whole(sign)],
                far_s.at[s, sign, 1], far_r.at[s, sign, 1], toward(sign, 2),
            )
            send(
                proj_sum.at[s, place(sign, 3)], far_in.at[s, sign, 0],
                far_s.at[s, sign, 0], far_r.at[s, sign, 0], toward(sign, 1),
            )

    def sum_near(s):
        for sign in range(2):
            send(
                proj_sum.at[s, place(sign, 1)], near_in.at[s, sign],
                near_s.at[s, sign], near_r.at[s, sign], toward(sign, 1),
            )

    def sum_mid(s):
        for sign in range(2):
            arrived(far_in.at[s, sign, 1, whole(sign)], far_r.at[s, sign, 1])
            arrived(far_in.at[s, sign, 0], far_r.at[s, sign, 0])
            mid_out[s, sign] = proj_sum[s, place(sign, 2)] + far_in[s, sign, 0]
            mid_out[s, sign, whole(sign)] = mid_out[s, sign, whole(sign)] + far_in[s, sign, 1, whole(sign)]
            send(
                mid_out.at[s, sign], mid_in.at[s, sign],
                mid_s.at[s, sign], mid_r.at[s, sign], toward(sign, 2),
            )

    def finish(s):
        total = proj_sum[s, order.index(0)]
        for sign in range(2):
            arrived(near_in.at[s, sign], near_r.at[s, sign])
            arrived(mid_in.at[s, sign], mid_r.at[s, sign])
            total = total + near_in[s, sign] + mid_in[s, sign]
        out_ref[:, s * PANEL:(s + 1) * PANEL] = total

    handle(0, 0)
    load_matrix.wait()
    do(matrix_work, 1)
    handle(0, 1)
    do(matrix_work, 2)
    handle(0, 2)
    do(matrix_work, 2)
    handle(0, 3)
    handle(1, 0)
    do(matrix_work, 2)
    handle(0, 4)
    do(matrix_work, 1)
    handle(1, 1)
    do(basis_work, 2)
    handle(1, 2)
    do(basis_work, 2)
    handle(1, 3)
    share(0, 0)
    share(0, 1)
    handle(1, 4)
    multiply(0, core, True)
    multiply(0, 2 + core, False)
    shared(0, 0)
    multiply(0, 1 - core, False)
    shared(0, 1)
    multiply(0, 3 - core, False)
    swap(0, 0)
    swap(0, 1)
    do(basis_work, 4)
    share(1, 0)
    share(1, 1)
    multiply(1, core, True)
    multiply(1, 2 + core, False)
    shared(1, 0)
    multiply(1, 1 - core, False)
    shared(1, 1)
    multiply(1, 3 - core, False)
    swap(1, 0)
    swap(1, 1)
    add_swap(0, 0)
    add_swap(0, 1)
    do(basis_work, len(basis_work))
    begin(0)
    exchange(0, 0)
    combine(0, 0)
    sum_far(0)
    add_swap(1, 0)
    exchange(0, 1)
    combine(0, 1)
    add_swap(1, 1)
    sum_mid(0)
    sum_near(0)
    begin(1)
    exchange(1, 0)
    combine(1, 0)
    sum_far(1)
    exchange(1, 1)
    combine(1, 1)
    sum_mid(1)
    sum_near(1)
    finish(0)
    finish(1)

    for copy in sends:
        copy.wait_send()
    for target, copy in cross:
        @pl.when(target != col)
        def _(copy=copy):
            copy.wait_send()


def body(matrix, basis_matrix, panel_index):
    rows, cols = matrix.shape
    piece = cols // (2 * PLANES)
    carried = rows // 2
    vmem = pltpu.VMEM

    def pairs(*shape):
        return [pltpu.SemaphoreType.DMA(shape), pltpu.SemaphoreType.DMA(shape)]

    return pl.pallas_call(
        kernel,
        out_shape=jax.ShapeDtypeStruct((piece, 2 * PANEL), F32),
        in_specs=[
            pl.BlockSpec(memory_space=pltpu.SMEM),
            pl.BlockSpec(memory_space=pl.ANY),
            pl.BlockSpec(memory_space=pl.ANY),
        ],
        out_specs=pl.BlockSpec(memory_space=pltpu.VMEM),
        scratch_shapes=[
            vmem((rows, cols), F32),
            vmem((rows, cols), F32),
            vmem((rows, cols), BF16),
            vmem((rows, cols), BF16),
            vmem((cols, rows), BF16),
            vmem((cols, rows), BF16),
            vmem((PASSES, carried, PANEL), F32),
            vmem((PASSES, carried, PANEL), F32),
            vmem((PLANES, PASSES, carried, PANEL), F32),
            vmem((4, COLS, rows, PANEL), F32),
            vmem((rows, 2 * PANEL), BF16),
            vmem((rows, 2 * PANEL), BF16),
            vmem((PASSES, rows, PANEL), BF16),
            vmem((PASSES, rows, PANEL), BF16),
            vmem((PASSES, 2, rows, PANEL), F32),
            vmem((PASSES, rows, PANEL), F32),
            vmem((PASSES, rows, PANEL), F32),
            vmem((PASSES, rows, PANEL), F32),
            vmem((PASSES, 2, PLANES, piece, PANEL), F32),
            vmem((PASSES, PLANES, piece, PANEL), F32),
            vmem((PASSES, PLANES, piece, PANEL), F32),
            vmem((PASSES, 2, 2, piece, PANEL), F32),
            vmem((PASSES, 2, piece, PANEL), F32),
            vmem((PASSES, 2, piece, PANEL), F32),
            vmem((PASSES, 2, piece, PANEL), F32),
            pltpu.SemaphoreType.DMA((2,)),
            *pairs(PASSES, UNITS),
            *pairs(4, PASSES, UNITS),
            *pairs(4, PASSES, UNITS),
            pltpu.SemaphoreType.DMA((PLANES, PASSES, PARTS)),
            pltpu.SemaphoreType.DMA((2, PASSES, COLS, PARTS)),
            *pairs(2, PASSES, COLS, PARTS),
            *pairs(PASSES, 2),
            *pairs(PASSES, 2),
            *pairs(PASSES, 2),
            *pairs(PASSES, 2, 2),
            *pairs(PASSES, 2),
            *pairs(PASSES, 2),
        ],
        compiler_params=pltpu.CompilerParams(
            collective_id=0, has_side_effects=True, vmem_limit_bytes=56 * 2**20
        ),
        name="project_panels",
    )(panel_index, matrix, basis_matrix)


def solution(mesh):
    return jax.shard_map(
        body,
        mesh=mesh,
        in_specs=(P(("grp", "row"), "col"), P(("grp", "row"), "col"), P("grp", None)),
        out_specs=P(("grp", "col", "row"), None),
        check_vma=False,
    )
```

```python
import functools

import jax
import jax.numpy as jnp
from jax import lax
from jax.experimental import pallas as pl
from jax.experimental.pallas import tpu as pltpu
from jax.sharding import PartitionSpec as P

PANEL = 128
MESH = pl.DeviceIdType.MESH
PLANES = 8
COLS = 4
PASSES = 2
UNITS = 4
PARTS = 2
SWAPS = 4
BF16 = jnp.bfloat16
F32 = jnp.float32


def split(value):
    high = value.astype(BF16)
    return high, (value - high.astype(F32)).astype(BF16)


def dot3(a_high, a_low, b_high, b_low):
    total = jnp.dot(a_high, b_high, preferred_element_type=F32)
    total += jnp.dot(a_high, b_low, preferred_element_type=F32)
    total += jnp.dot(a_low, b_high, preferred_element_type=F32)
    return total


def kernel(
    index_ref, matrix_hbm, basis_hbm, out_ref,
    matrix_v, basis_v, m_high, m_low, qt_high, qt_low,
    pair_out, pair_in, ring, chosen, x_high, x_low, y_high, y_low,
    image, image_in, image_sum, image_pair,
    proj, proj_in, proj_sum, far_in, mid_out, mid_in, near_in,
    load_sem, pair_s, pair_r, up_s, up_r, down_s, down_r,
    cross_s, cross_r, twin_s, twin_r, swap_s, swap_r, half_s, half_r,
    mate_s, mate_r, far_s, far_r, mid_s, mid_r, near_s, near_r,
):
    grp = lax.axis_index("grp")
    row = lax.axis_index("row")
    col = lax.axis_index("col")
    plane = row // 2
    core = lax.rem(row, 2)
    half = col // 2
    slot = lax.rem(col, 2)
    rows = basis_v.shape[0]
    cols = basis_v.shape[1]
    piece = cols // (2 * PLANES)
    per_col = cols // PANEL
    carried = rows // 2
    unit = carried // UNITS
    portion = carried // PARTS

    def at(r, c):
        return (grp, r, c)

    def along(step):
        return at(lax.rem(plane + PLANES + step, PLANES) * 2 + core, col)

    twin = at(row + 1 - 2 * core, col)
    above = along(1)
    below = along(-1)
    pair = at(row, col + 1 - 2 * slot)
    mirror = at(row, 3 - col)
    across = at(row, lax.rem(col + 2, COLS))

    load_basis = pltpu.make_async_copy(basis_hbm, basis_v, load_sem.at[0])
    load_matrix = pltpu.make_async_copy(matrix_hbm, matrix_v, load_sem.at[1])
    load_basis.start()

    barrier = pltpu.get_barrier_semaphore()
    partners = (twin, above, below, along(2), along(-2), pair, mirror, across)
    for other in partners:
        pl.semaphore_signal(barrier, inc=1, device_id=other, device_id_type=MESH)

    sends = []

    def send(src, dst, send_sem, recv_sem, target):
        copy = pltpu.make_async_remote_copy(
            src_ref=src, dst_ref=dst, send_sem=send_sem, recv_sem=recv_sem,
            device_id=target, device_id_type=MESH,
        )
        copy.start()
        sends.append(copy)

    def arrived(ref, sem):
        pltpu.make_async_copy(ref, ref, sem).wait()

    load_basis.wait()
    load_matrix.start()
    span_rows = min(64, carried)

    def pick(s, i, row_half):
        index = index_ref[half, s] - slot * per_col
        at_rows = pl.ds(pl.multiple_of(row_half * carried + i * span_rows, span_rows), span_rows)
        index_v = jnp.full((span_rows, PANEL), index, jnp.int32)
        total = jnp.zeros((span_rows, PANEL), F32)
        for j in range(per_col):
            total = jnp.where(index_v == j, basis_v[at_rows, j * PANEL:(j + 1) * PANEL], total)
        return total

    def pick_other(i, carry):
        for s in range(PASSES):
            at_rows = pl.ds(pl.multiple_of(i * span_rows, span_rows), span_rows)
            pair_out[s, at_rows] = pick(s, i, 1 - slot)
        return carry

    def pick_own(i, carry):
        for s in range(PASSES):
            at_rows = pl.ds(pl.multiple_of(i * span_rows, span_rows), span_rows)
            ring[0, s, at_rows] = pick(s, i, slot)
        return carry

    lax.fori_loop(0, carried // span_rows, pick_other, 0)
    pl.semaphore_wait(barrier, len(partners))

    def of_unit(u):
        return pl.ds(u * unit, unit)

    def of_portion(v):
        return pl.ds(v * portion, portion)

    for s in range(PASSES):
        for u in range(UNITS):
            send(
                pair_out.at[s, of_unit(u)], pair_in.at[s, of_unit(u)],
                pair_s.at[s, u], pair_r.at[s, u], pair,
            )
    lax.fori_loop(0, carried // span_rows, pick_own, 0)

    def split_matrix(b):
        at_cols = pl.ds(b * 2 * PANEL, 2 * PANEL)
        m_high[:, at_cols], m_low[:, at_cols] = split(matrix_v[:, at_cols])

    def split_basis(b):
        at_cols = pl.ds(b * PANEL, PANEL)
        qt_high[at_cols, :], qt_low[at_cols, :] = split(basis_v[:, at_cols].T)

    matrix_work = [functools.partial(split_matrix, b) for b in range(cols // (2 * PANEL))]
    basis_work = [functools.partial(split_basis, b) for b in range(cols // PANEL)]

    def do(work, count):
        for _ in range(min(count, len(work))):
            work.pop(0)()

    cross = []

    def deliver(s, d, v):
        source = lax.rem(plane + PLANES - d, PLANES)
        target = source // 2
        odd = lax.rem(source, 2)
        src = ring.at[d, s, of_portion(v)]
        first = pl.multiple_of(slot * carried + v * portion, portion)
        dst = chosen.at[2 * odd + core, 2 * half + s, pl.ds(first, portion)]
        sem = cross_r.at[odd, s, col, v]
        copy = pltpu.make_async_remote_copy(
            src_ref=src, dst_ref=dst, send_sem=cross_s.at[d, s, v], recv_sem=sem,
            device_id=at(row, target), device_id_type=MESH,
        )

        @pl.when(target != col)
        def _():
            copy.start()

        @pl.when(target == col)
        def _():
            pltpu.make_async_copy(src, dst, sem).start()

        cross.append((target, copy))

    def go_up(s, d, u):
        send(
            ring.at[d, s, of_unit(u)], ring.at[d + 1, s, of_unit(u)],
            up_s.at[d, s, u], up_r.at[d, s, u], above,
        )

    def go_down(s, d, u):
        send(
            ring.at[(PLANES - d) % PLANES, s, of_unit(u)],
            ring.at[PLANES - 1 - d, s, of_unit(u)],
            down_s.at[d, s, u], down_r.at[d, s, u], below,
        )

    def handle(s, d):
        for u in range(UNITS):
            up_far, down_far = u % 2 == 0, u % 2 == 1
            if d == 0:
                arrived(pair_in.at[s, of_unit(u)], pair_r.at[s, u])
                ring[0, s, of_unit(u)] = ring[0, s, of_unit(u)] + pair_in[s, of_unit(u)]
                go_up(s, 0, u)
                go_down(s, 0, u)
            if d > 0 and (d < 4 or up_far):
                arrived(ring.at[d, s, of_unit(u)], up_r.at[d - 1, s, u])
                if d < 3 or (d == 3 and up_far):
                    go_up(s, d, u)
            if d > 0 and (d < 4 or down_far):
                arrived(ring.at[PLANES - d, s, of_unit(u)], down_r.at[d - 1, s, u])
                if d < 3 or (d == 3 and down_far):
                    go_down(s, d, u)
            if u % 2 == 1:
                deliver(s, d, u // 2)
                if 0 < d < 4:
                    deliver(s, PLANES - d, u // 2)

    def share(s, odd):
        for v in range(PARTS):
            for c in range(COLS):
                first = (c % 2) * carried + v * portion
                ref = chosen.at[2 * odd + core, 2 * (c // 2) + s, pl.ds(first, portion)]
                arrived(ref, cross_r.at[odd, s, c, v])
                send(ref, ref, twin_s.at[odd, s, c, v], twin_r.at[odd, s, c, v], twin)

    def shared(s, odd):
        for v in range(PARTS):
            for c in range(COLS):
                first = (c % 2) * carried + v * portion
                ref = chosen.at[2 * odd + 1 - core, 2 * (c // 2) + s, pl.ds(first, portion)]
                arrived(ref, twin_r.at[odd, s, c, v])

    def multiply(s, block, first):
        value = jnp.concatenate([chosen[block, s], chosen[block, 2 + s]], axis=1)
        x_high[...], x_low[...] = split(value)
        at_cols = pl.ds(pl.multiple_of(block * rows, rows), rows)

        def body(i, carry):
            at_rows = pl.ds(pl.multiple_of(i * carried, carried), carried)
            term = dot3(m_high[at_rows, at_cols], m_low[at_rows, at_cols], x_high[...], x_low[...])
            for h in range(2):
                piece_h = term[:, h * PANEL:(h + 1) * PANEL]
                image[s, h, at_rows] = piece_h if first else image[s, h, at_rows] + piece_h
            return carry
        lax.fori_loop(0, 2, body, 0)

    def half_rows(v):
        return pl.ds(v * (rows // SWAPS), rows // SWAPS)

    def swap(s, v):
        send(
            image.at[s, 1 - half, half_rows(v)], image_in.at[s, half_rows(v)],
            swap_s.at[s, v], swap_r.at[s, v], mirror,
        )

    def add_swap(s, v):
        at_rows = half_rows(v)
        arrived(image_in.at[s, at_rows], swap_r.at[s, v])
        image_sum[s, at_rows] = image[s, half, at_rows] + image_in[s, at_rows]
        send(
            image_sum.at[s, at_rows], image_pair.at[s, at_rows],
            half_s.at[s, v], half_r.at[s, v], pair,
        )

    order = (4, 3, 5, 2, 6, 1, 7, 0)
    groups = ((0, 3), (3, 8))

    def project(s, parity, group):
        for i in range(*groups[group]):
            target = lax.rem(plane + order[i], PLANES)
            at_rows = pl.ds(pl.multiple_of((2 * target + parity) * piece, piece), piece)
            proj[s, parity, i] = dot3(
                qt_high[at_rows, :], qt_low[at_rows, :], y_high[s], y_low[s]
            )

    def begin(s):
        for v in range(SWAPS):
            arrived(image_pair.at[s, half_rows(v)], half_r.at[s, v])
        y_high[s], y_low[s] = split(image_sum[s] + image_pair[s])

    def exchange(s, group):
        first, last = groups[group]
        span_i = pl.ds(first, last - first)
        project(s, 1 - core, group)
        send(
            proj.at[s, 1 - core, span_i], proj_in.at[s, span_i],
            mate_s.at[s, group], mate_r.at[s, group], twin,
        )
        project(s, core, group)

    def combine(s, group):
        first, last = groups[group]
        span_i = pl.ds(first, last - first)
        arrived(proj_in.at[s, span_i], mate_r.at[s, group])
        proj_sum[s, span_i] = proj[s, core, span_i] + proj_in[s, span_i]

    near_rows = piece // 2

    def whole(sign):
        return pl.ds(0, near_rows) if sign == 0 else pl.ds(near_rows, near_rows)

    def place(sign, d):
        return order.index(d if sign == 0 else PLANES - d)

    def toward(sign, d):
        return along(d if sign == 0 else -d)

    def sum_far(s):
        for sign in range(2):
            send(
                proj_sum.at[s, place(sign, 4), whole(sign)], far_in.at[s, sign, 1, whole(sign)],
                far_s.at[s, sign, 1], far_r.at[s, sign, 1], toward(sign, 2),
            )
            send(
                proj_sum.at[s, place(sign, 3)], far_in.at[s, sign, 0],
                far_s.at[s, sign, 0], far_r.at[s, sign, 0], toward(sign, 1),
            )

    def sum_near(s):
        for sign in range(2):
            send(
                proj_sum.at[s, place(sign, 1)], near_in.at[s, sign],
                near_s.at[s, sign], near_r.at[s, sign], toward(sign, 1),
            )

    def sum_mid(s):
        for sign in range(2):
            arrived(far_in.at[s, sign, 1, whole(sign)], far_r.at[s, sign, 1])
            arrived(far_in.at[s, sign, 0], far_r.at[s, sign, 0])
            mid_out[s, sign] = proj_sum[s, place(sign, 2)] + far_in[s, sign, 0]
            mid_out[s, sign, whole(sign)] = mid_out[s, sign, whole(sign)] + far_in[s, sign, 1, whole(sign)]
            send(
                mid_out.at[s, sign], mid_in.at[s, sign],
                mid_s.at[s, sign], mid_r.at[s, sign], toward(sign, 2),
            )

    def finish(s):
        total = proj_sum[s, order.index(0)]
        for sign in range(2):
            arrived(near_in.at[s, sign], near_r.at[s, sign])
            arrived(mid_in.at[s, sign], mid_r.at[s, sign])
            total = total + near_in[s, sign] + mid_in[s, sign]
        out_ref[:, s * PANEL:(s + 1) * PANEL] = total

    handle(0, 0)
    load_matrix.wait()
    do(matrix_work, 2)
    handle(0, 1)
    do(matrix_work, 2)
    handle(0, 2)
    do(matrix_work, 2)
    handle(1, 0)
    do(matrix_work, 2)
    handle(0, 3)
    do(basis_work, 0)
    handle(1, 1)
    do(basis_work, 0)
    handle(0, 4)
    do(basis_work, 0)
    handle(1, 2)
    do(basis_work, 0)
    handle(1, 3)
    do(basis_work, 0)
    handle(1, 4)
    do(basis_work, 0)
    share(0, 0)
    share(0, 1)
    multiply(0, core, True)
    multiply(0, 2 + core, False)
    shared(0, 0)
    multiply(0, 1 - core, False)
    shared(0, 1)
    multiply(0, 3 - core, False)
    swap(0, 0)
    swap(0, 1)
    swap(0, 2)
    swap(0, 3)
    share(1, 0)
    share(1, 1)
    multiply(1, core, True)
    multiply(1, 2 + core, False)
    add_swap(0, 0)
    add_swap(0, 1)
    add_swap(0, 2)
    add_swap(0, 3)
    shared(1, 0)
    multiply(1, 1 - core, False)
    shared(1, 1)
    multiply(1, 3 - core, False)
    swap(1, 0)
    swap(1, 1)
    swap(1, 2)
    swap(1, 3)
    do(basis_work, 16)
    begin(0)
    exchange(0, 0)
    combine(0, 0)
    sum_far(0)
    add_swap(1, 0)
    add_swap(1, 1)
    exchange(0, 1)
    add_swap(1, 2)
    add_swap(1, 3)
    combine(0, 1)
    sum_near(0)
    sum_mid(0)
    begin(1)
    exchange(1, 0)
    combine(1, 0)
    sum_far(1)
    exchange(1, 1)
    combine(1, 1)
    sum_near(1)
    sum_mid(1)
    finish(0)
    finish(1)
    for copy in sends:
        copy.wait_send()
    for target, copy in cross:
        @pl.when(target != col)
        def _(copy=copy):
            copy.wait_send()


def body(matrix, basis_matrix, panel_index):
    rows, cols = matrix.shape
    piece = cols // (2 * PLANES)
    carried = rows // 2
    vmem = pltpu.VMEM

    def pairs(*shape):
        return [pltpu.SemaphoreType.DMA(shape), pltpu.SemaphoreType.DMA(shape)]

    return pl.pallas_call(
        kernel,
        out_shape=jax.ShapeDtypeStruct((piece, 2 * PANEL), F32),
        in_specs=[
            pl.BlockSpec(memory_space=pltpu.SMEM),
            pl.BlockSpec(memory_space=pl.ANY),
            pl.BlockSpec(memory_space=pl.ANY),
        ],
        out_specs=pl.BlockSpec(memory_space=pltpu.VMEM),
        scratch_shapes=[
            vmem((rows, cols), F32),
            vmem((rows, cols), F32),
            vmem((rows, cols), BF16),
            vmem((rows, cols), BF16),
            vmem((cols, rows), BF16),
            vmem((cols, rows), BF16),
            vmem((PASSES, carried, PANEL), F32),
            vmem((PASSES, carried, PANEL), F32),
            vmem((PLANES, PASSES, carried, PANEL), F32),
            vmem((4, COLS, rows, PANEL), F32),
            vmem((rows, 2 * PANEL), BF16),
            vmem((rows, 2 * PANEL), BF16),
            vmem((PASSES, rows, PANEL), BF16),
            vmem((PASSES, rows, PANEL), BF16),
            vmem((PASSES, 2, rows, PANEL), F32),
            vmem((PASSES, rows, PANEL), F32),
            vmem((PASSES, rows, PANEL), F32),
            vmem((PASSES, rows, PANEL), F32),
            vmem((PASSES, 2, PLANES, piece, PANEL), F32),
            vmem((PASSES, PLANES, piece, PANEL), F32),
            vmem((PASSES, PLANES, piece, PANEL), F32),
            vmem((PASSES, 2, 2, piece, PANEL), F32),
            vmem((PASSES, 2, piece, PANEL), F32),
            vmem((PASSES, 2, piece, PANEL), F32),
            vmem((PASSES, 2, piece, PANEL), F32),
            pltpu.SemaphoreType.DMA((2,)),
            *pairs(PASSES, UNITS),
            *pairs(4, PASSES, UNITS),
            *pairs(4, PASSES, UNITS),
            pltpu.SemaphoreType.DMA((PLANES, PASSES, PARTS)),
            pltpu.SemaphoreType.DMA((2, PASSES, COLS, PARTS)),
            *pairs(2, PASSES, COLS, PARTS),
            *pairs(PASSES, SWAPS),
            *pairs(PASSES, SWAPS),
            *pairs(PASSES, 2),
            *pairs(PASSES, 2, 2),
            *pairs(PASSES, 2),
            *pairs(PASSES, 2),
        ],
        compiler_params=pltpu.CompilerParams(
            collective_id=0, has_side_effects=True, vmem_limit_bytes=56 * 2**20
        ),
        name="project_panels",
    )(panel_index, matrix, basis_matrix)


def solution(mesh):
    return jax.shard_map(
        body,
        mesh=mesh,
        in_specs=(P(("grp", "row"), "col"), P(("grp", "row"), "col"), P("grp", None)),
        out_specs=P(("grp", "col", "row"), None),
        check_vma=False,
    )
```

```python
import functools

import jax
import jax.numpy as jnp
from jax import lax
from jax.experimental import pallas as pl
from jax.experimental.pallas import tpu as pltpu
from jax.sharding import PartitionSpec as P

PANEL = 128
MESH = pl.DeviceIdType.MESH
PLANES = 8
COLS = 4
PASSES = 2
UNITS = 4
PARTS = 2
SWAPS = 4
BF16 = jnp.bfloat16
F32 = jnp.float32


def split(value):
    high = value.astype(BF16)
    return high, (value - high.astype(F32)).astype(BF16)


def dot3(a_high, a_low, b_high, b_low):
    total = jnp.dot(a_high, b_high, preferred_element_type=F32)
    total += jnp.dot(a_high, b_low, preferred_element_type=F32)
    total += jnp.dot(a_low, b_high, preferred_element_type=F32)
    return total


def kernel(
    index_ref, matrix_hbm, basis_hbm, out_ref,
    matrix_v, basis_v, m_high, m_low, qt_high, qt_low,
    pair_out, pair_in, ring, chosen, x_high, x_low, y_high, y_low,
    image, image_in, image_sum, image_pair,
    proj, proj_in, proj_sum, far_in, mid_out, mid_in, near_in,
    load_sem, pair_s, pair_r, up_s, up_r, down_s, down_r,
    cross_s, cross_r, twin_s, twin_r, swap_s, swap_r, half_s, half_r,
    mate_s, mate_r, far_s, far_r, mid_s, mid_r, near_s, near_r,
):
    grp = lax.axis_index("grp")
    row = lax.axis_index("row")
    col = lax.axis_index("col")
    plane = row // 2
    core = lax.rem(row, 2)
    half = col // 2
    slot = lax.rem(col, 2)
    rows = basis_v.shape[0]
    cols = basis_v.shape[1]
    piece = cols // (2 * PLANES)
    per_col = cols // PANEL
    carried = rows // 2
    unit = carried // UNITS
    portion = carried // PARTS

    def at(r, c):
        return (grp, r, c)

    def along(step):
        return at(lax.rem(plane + PLANES + step, PLANES) * 2 + core, col)

    twin = at(row + 1 - 2 * core, col)
    above = along(1)
    below = along(-1)
    pair = at(row, col + 1 - 2 * slot)
    mirror = at(row, 3 - col)
    across = at(row, lax.rem(col + 2, COLS))

    def load_half(which, row_half):
        at_rows = pl.ds(pl.multiple_of(row_half * carried, carried), carried)
        return pltpu.make_async_copy(
            basis_hbm.at[at_rows], basis_v.at[at_rows], load_sem.at[which]
        )

    load_other = load_half(0, 1 - slot)
    load_own = load_half(2, slot)
    load_matrix = pltpu.make_async_copy(matrix_hbm, matrix_v, load_sem.at[1])
    load_other.start()
    load_own.start()

    barrier = pltpu.get_barrier_semaphore()
    partners = (twin, above, below, along(2), along(-2), pair, mirror, across)
    for other in partners:
        pl.semaphore_signal(barrier, inc=1, device_id=other, device_id_type=MESH)

    sends = []

    def send(src, dst, send_sem, recv_sem, target):
        copy = pltpu.make_async_remote_copy(
            src_ref=src, dst_ref=dst, send_sem=send_sem, recv_sem=recv_sem,
            device_id=target, device_id_type=MESH,
        )
        copy.start()
        sends.append(copy)

    def arrived(ref, sem):
        pltpu.make_async_copy(ref, ref, sem).wait()

    load_other.wait()
    span_rows = min(64, carried)

    def pick(s, i, row_half):
        index = index_ref[half, s] - slot * per_col
        at_rows = pl.ds(pl.multiple_of(row_half * carried + i * span_rows, span_rows), span_rows)
        index_v = jnp.full((span_rows, PANEL), index, jnp.int32)
        total = jnp.zeros((span_rows, PANEL), F32)
        for j in range(per_col):
            total = jnp.where(index_v == j, basis_v[at_rows, j * PANEL:(j + 1) * PANEL], total)
        return total

    def pick_into(ref, s, row_half):
        def body(i, carry):
            at_rows = pl.ds(pl.multiple_of(i * span_rows, span_rows), span_rows)
            ref[s, at_rows] = pick(s, i, row_half)
            return carry
        lax.fori_loop(0, carried // span_rows, body, 0)

    pick_into(pair_out, 0, 1 - slot)
    pl.semaphore_wait(barrier, len(partners))

    def of_unit(u):
        return pl.ds(u * unit, unit)

    def of_portion(v):
        return pl.ds(v * portion, portion)

    def exchange_pair(s):
        for u in range(UNITS):
            send(
                pair_out.at[s, of_unit(u)], pair_in.at[s, of_unit(u)],
                pair_s.at[s, u], pair_r.at[s, u], pair,
            )

    exchange_pair(0)
    load_own.wait()
    load_matrix.start()
    pick_into(ring.at[0], 0, slot)
    pick_into(pair_out, 1, 1 - slot)
    pick_into(ring.at[0], 1, slot)

    def split_matrix(b):
        at_cols = pl.ds(b * 2 * PANEL, 2 * PANEL)
        m_high[:, at_cols], m_low[:, at_cols] = split(matrix_v[:, at_cols])

    def split_basis(b):
        at_cols = pl.ds(b * PANEL, PANEL)
        qt_high[at_cols, :], qt_low[at_cols, :] = split(basis_v[:, at_cols].T)

    matrix_work = [functools.partial(split_matrix, b) for b in range(cols // (2 * PANEL))]
    basis_work = [functools.partial(split_basis, b) for b in range(cols // PANEL)]

    def do(work, count):
        for _ in range(min(count, len(work))):
            work.pop(0)()

    cross = []

    def deliver(s, d, v):
        source = lax.rem(plane + PLANES - d, PLANES)
        target = source // 2
        odd = lax.rem(source, 2)
        src = ring.at[d, s, of_portion(v)]
        first = pl.multiple_of(slot * carried + v * portion, portion)
        dst = chosen.at[2 * odd + core, 2 * half + s, pl.ds(first, portion)]
        sem = cross_r.at[odd, s, col, v]
        copy = pltpu.make_async_remote_copy(
            src_ref=src, dst_ref=dst, send_sem=cross_s.at[d, s, v], recv_sem=sem,
            device_id=at(row, target), device_id_type=MESH,
        )

        @pl.when(target != col)
        def _():
            copy.start()

        @pl.when(target == col)
        def _():
            pltpu.make_async_copy(src, dst, sem).start()

        cross.append((target, copy))

    def go_up(s, d, u):
        send(
            ring.at[d, s, of_unit(u)], ring.at[d + 1, s, of_unit(u)],
            up_s.at[d, s, u], up_r.at[d, s, u], above,
        )

    def go_down(s, d, u):
        send(
            ring.at[(PLANES - d) % PLANES, s, of_unit(u)],
            ring.at[PLANES - 1 - d, s, of_unit(u)],
            down_s.at[d, s, u], down_r.at[d, s, u], below,
        )

    def handle(s, d):
        for u in range(UNITS):
            up_far, down_far = u % 2 == 0, u % 2 == 1
            if d == 0:
                arrived(pair_in.at[s, of_unit(u)], pair_r.at[s, u])
                ring[0, s, of_unit(u)] = ring[0, s, of_unit(u)] + pair_in[s, of_unit(u)]
                go_up(s, 0, u)
                go_down(s, 0, u)
            if d > 0 and (d < 4 or up_far):
                arrived(ring.at[d, s, of_unit(u)], up_r.at[d - 1, s, u])
                if d < 3 or (d == 3 and up_far):
                    go_up(s, d, u)
            if d > 0 and (d < 4 or down_far):
                arrived(ring.at[PLANES - d, s, of_unit(u)], down_r.at[d - 1, s, u])
                if d < 3 or (d == 3 and down_far):
                    go_down(s, d, u)
            if u % 2 == 1:
                deliver(s, d, u // 2)
                if 0 < d < 4:
                    deliver(s, PLANES - d, u // 2)

    def share(s, odd):
        for v in range(PARTS):
            for c in range(COLS):
                first = (c % 2) * carried + v * portion
                ref = chosen.at[2 * odd + core, 2 * (c // 2) + s, pl.ds(first, portion)]
                arrived(ref, cross_r.at[odd, s, c, v])
                send(ref, ref, twin_s.at[odd, s, c, v], twin_r.at[odd, s, c, v], twin)

    def shared(s, odd):
        for v in range(PARTS):
            for c in range(COLS):
                first = (c % 2) * carried + v * portion
                ref = chosen.at[2 * odd + 1 - core, 2 * (c // 2) + s, pl.ds(first, portion)]
                arrived(ref, twin_r.at[odd, s, c, v])

    def multiply(s, block, first):
        value = jnp.concatenate([chosen[block, s], chosen[block, 2 + s]], axis=1)
        x_high[...], x_low[...] = split(value)
        at_cols = pl.ds(pl.multiple_of(block * rows, rows), rows)

        def body(i, carry):
            at_rows = pl.ds(pl.multiple_of(i * carried, carried), carried)
            term = dot3(m_high[at_rows, at_cols], m_low[at_rows, at_cols], x_high[...], x_low[...])
            for h in range(2):
                piece_h = term[:, h * PANEL:(h + 1) * PANEL]
                image[s, h, at_rows] = piece_h if first else image[s, h, at_rows] + piece_h
            return carry
        lax.fori_loop(0, 2, body, 0)

    def half_rows(v):
        return pl.ds(v * (rows // SWAPS), rows // SWAPS)

    def swap(s, v):
        send(
            image.at[s, 1 - half, half_rows(v)], image_in.at[s, half_rows(v)],
            swap_s.at[s, v], swap_r.at[s, v], mirror,
        )

    def add_swap(s, v):
        at_rows = half_rows(v)
        arrived(image_in.at[s, at_rows], swap_r.at[s, v])
        image_sum[s, at_rows] = image[s, half, at_rows] + image_in[s, at_rows]
        send(
            image_sum.at[s, at_rows], image_pair.at[s, at_rows],
            half_s.at[s, v], half_r.at[s, v], pair,
        )

    order = (4, 3, 5, 2, 6, 1, 7, 0)
    groups = ((0, 3), (3, 8))

    def project(s, parity, group):
        for i in range(*groups[group]):
            target = lax.rem(plane + order[i], PLANES)
            at_rows = pl.ds(pl.multiple_of((2 * target + parity) * piece, piece), piece)
            proj[s, parity, i] = dot3(
                qt_high[at_rows, :], qt_low[at_rows, :], y_high[s], y_low[s]
            )

    def begin(s):
        for v in range(SWAPS):
            arrived(image_pair.at[s, half_rows(v)], half_r.at[s, v])
        y_high[s], y_low[s] = split(image_sum[s] + image_pair[s])

    def exchange(s, group):
        first, last = groups[group]
        span_i = pl.ds(first, last - first)
        project(s, 1 - core, group)
        send(
            proj.at[s, 1 - core, span_i], proj_in.at[s, span_i],
            mate_s.at[s, group], mate_r.at[s, group], twin,
        )
        project(s, core, group)

    def combine(s, group):
        first, last = groups[group]
        span_i = pl.ds(first, last - first)
        arrived(proj_in.at[s, span_i], mate_r.at[s, group])
        proj_sum[s, span_i] = proj[s, core, span_i] + proj_in[s, span_i]

    near_rows = piece // 2

    def whole(sign):
        return pl.ds(0, near_rows) if sign == 0 else pl.ds(near_rows, near_rows)

    def place(sign, d):
        return order.index(d if sign == 0 else PLANES - d)

    def toward(sign, d):
        return along(d if sign == 0 else -d)

    def sum_far(s):
        for sign in range(2):
            send(
                proj_sum.at[s, place(sign, 4), whole(sign)], far_in.at[s, sign, 1, whole(sign)],
                far_s.at[s, sign, 1], far_r.at[s, sign, 1], toward(sign, 2),
            )
            send(
                proj_sum.at[s, place(sign, 3)], far_in.at[s, sign, 0],
                far_s.at[s, sign, 0], far_r.at[s, sign, 0], toward(sign, 1),
            )

    def sum_near(s):
        for sign in range(2):
            send(
                proj_sum.at[s, place(sign, 1)], near_in.at[s, sign],
                near_s.at[s, sign], near_r.at[s, sign], toward(sign, 1),
            )

    def sum_mid(s):
        for sign in range(2):
            arrived(far_in.at[s, sign, 1, whole(sign)], far_r.at[s, sign, 1])
            arrived(far_in.at[s, sign, 0], far_r.at[s, sign, 0])
            mid_out[s, sign] = proj_sum[s, place(sign, 2)] + far_in[s, sign, 0]
            mid_out[s, sign, whole(sign)] = mid_out[s, sign, whole(sign)] + far_in[s, sign, 1, whole(sign)]
            send(
                mid_out.at[s, sign], mid_in.at[s, sign],
                mid_s.at[s, sign], mid_r.at[s, sign], toward(sign, 2),
            )

    def finish(s):
        total = proj_sum[s, order.index(0)]
        for sign in range(2):
            arrived(near_in.at[s, sign], near_r.at[s, sign])
            arrived(mid_in.at[s, sign], mid_r.at[s, sign])
            total = total + near_in[s, sign] + mid_in[s, sign]
        out_ref[:, s * PANEL:(s + 1) * PANEL] = total

    handle(0, 0)
    exchange_pair(1)
    load_matrix.wait()
    do(matrix_work, 2)
    handle(0, 1)
    do(matrix_work, 2)
    handle(0, 2)
    do(matrix_work, 2)
    handle(1, 0)
    do(matrix_work, 2)
    handle(0, 3)
    do(basis_work, 0)
    handle(1, 1)
    do(basis_work, 0)
    handle(0, 4)
    do(basis_work, 0)
    handle(1, 2)
    do(basis_work, 0)
    handle(1, 3)
    do(basis_work, 0)
    handle(1, 4)
    do(basis_work, 0)
    share(0, 0)
    share(0, 1)
    multiply(0, core, True)
    multiply(0, 2 + core, False)
    shared(0, 0)
    multiply(0, 1 - core, False)
    shared(0, 1)
    multiply(0, 3 - core, False)
    swap(0, 0)
    swap(0, 1)
    swap(0, 2)
    swap(0, 3)
    share(1, 0)
    share(1, 1)
    multiply(1, core, True)
    multiply(1, 2 + core, False)
    add_swap(0, 0)
    add_swap(0, 1)
    add_swap(0, 2)
    add_swap(0, 3)
    shared(1, 0)
    multiply(1, 1 - core, False)
    shared(1, 1)
    multiply(1, 3 - core, False)
    swap(1, 0)
    swap(1, 1)
    swap(1, 2)
    swap(1, 3)
    do(basis_work, 16)
    begin(0)
    exchange(0, 0)
    combine(0, 0)
    sum_far(0)
    add_swap(1, 0)
    add_swap(1, 1)
    exchange(0, 1)
    add_swap(1, 2)
    add_swap(1, 3)
    combine(0, 1)
    sum_near(0)
    sum_mid(0)
    begin(1)
    exchange(1, 0)
    combine(1, 0)
    sum_far(1)
    exchange(1, 1)
    combine(1, 1)
    sum_near(1)
    sum_mid(1)
    finish(0)
    finish(1)
    for copy in sends:
        copy.wait_send()
    for target, copy in cross:
        @pl.when(target != col)
        def _(copy=copy):
            copy.wait_send()


def body(matrix, basis_matrix, panel_index):
    rows, cols = matrix.shape
    piece = cols // (2 * PLANES)
    carried = rows // 2
    vmem = pltpu.VMEM

    def pairs(*shape):
        return [pltpu.SemaphoreType.DMA(shape), pltpu.SemaphoreType.DMA(shape)]

    return pl.pallas_call(
        kernel,
        out_shape=jax.ShapeDtypeStruct((piece, 2 * PANEL), F32),
        in_specs=[
            pl.BlockSpec(memory_space=pltpu.SMEM),
            pl.BlockSpec(memory_space=pl.ANY),
            pl.BlockSpec(memory_space=pl.ANY),
        ],
        out_specs=pl.BlockSpec(memory_space=pltpu.VMEM),
        scratch_shapes=[
            vmem((rows, cols), F32),
            vmem((rows, cols), F32),
            vmem((rows, cols), BF16),
            vmem((rows, cols), BF16),
            vmem((cols, rows), BF16),
            vmem((cols, rows), BF16),
            vmem((PASSES, carried, PANEL), F32),
            vmem((PASSES, carried, PANEL), F32),
            vmem((PLANES, PASSES, carried, PANEL), F32),
            vmem((4, COLS, rows, PANEL), F32),
            vmem((rows, 2 * PANEL), BF16),
            vmem((rows, 2 * PANEL), BF16),
            vmem((PASSES, rows, PANEL), BF16),
            vmem((PASSES, rows, PANEL), BF16),
            vmem((PASSES, 2, rows, PANEL), F32),
            vmem((PASSES, rows, PANEL), F32),
            vmem((PASSES, rows, PANEL), F32),
            vmem((PASSES, rows, PANEL), F32),
            vmem((PASSES, 2, PLANES, piece, PANEL), F32),
            vmem((PASSES, PLANES, piece, PANEL), F32),
            vmem((PASSES, PLANES, piece, PANEL), F32),
            vmem((PASSES, 2, 2, piece, PANEL), F32),
            vmem((PASSES, 2, piece, PANEL), F32),
            vmem((PASSES, 2, piece, PANEL), F32),
            vmem((PASSES, 2, piece, PANEL), F32),
            pltpu.SemaphoreType.DMA((3,)),
            *pairs(PASSES, UNITS),
            *pairs(4, PASSES, UNITS),
            *pairs(4, PASSES, UNITS),
            pltpu.SemaphoreType.DMA((PLANES, PASSES, PARTS)),
            pltpu.SemaphoreType.DMA((2, PASSES, COLS, PARTS)),
            *pairs(2, PASSES, COLS, PARTS),
            *pairs(PASSES, SWAPS),
            *pairs(PASSES, SWAPS),
            *pairs(PASSES, 2),
            *pairs(PASSES, 2, 2),
            *pairs(PASSES, 2),
            *pairs(PASSES, 2),
        ],
        compiler_params=pltpu.CompilerParams(
            collective_id=0, has_side_effects=True, vmem_limit_bytes=56 * 2**20
        ),
        name="project_panels",
    )(panel_index, matrix, basis_matrix)


def solution(mesh):
    return jax.shard_map(
        body,
        mesh=mesh,
        in_specs=(P(("grp", "row"), "col"), P(("grp", "row"), "col"), P("grp", None)),
        out_specs=P(("grp", "col", "row"), None),
        check_vma=False,
    )
```

```python
import functools

import jax
import jax.numpy as jnp
from jax import lax
from jax.experimental import pallas as pl
from jax.experimental.pallas import tpu as pltpu
from jax.sharding import PartitionSpec as P

PANEL = 128
MESH = pl.DeviceIdType.MESH
PLANES = 8
COLS = 4
PASSES = 2
UNITS = 4
PARTS = 2
SWAPS = 4
BF16 = jnp.bfloat16
F32 = jnp.float32


def split(value):
    high = value.astype(BF16)
    return high, (value - high.astype(F32)).astype(BF16)


def dot3(a_high, a_low, b_high, b_low):
    total = jnp.dot(a_high, b_high, preferred_element_type=F32)
    total += jnp.dot(a_high, b_low, preferred_element_type=F32)
    total += jnp.dot(a_low, b_high, preferred_element_type=F32)
    return total


def kernel(
    index_ref, matrix_hbm, basis_hbm, out_ref,
    matrix_v, basis_v, m_high, m_low, q_high, q_low,
    pair_out, pair_in, ring, chosen, x_high, x_low, y_high, y_low,
    image, image_in, image_sum, image_pair,
    proj, proj_in, proj_sum, far_in, mid_out, mid_in, near_in,
    load_sem, pair_s, pair_r, up_s, up_r, down_s, down_r,
    cross_s, cross_r, twin_s, twin_r, swap_s, swap_r, half_s, half_r,
    mate_s, mate_r, far_s, far_r, mid_s, mid_r, near_s, near_r,
):
    grp = lax.axis_index("grp")
    row = lax.axis_index("row")
    col = lax.axis_index("col")
    plane = row // 2
    core = lax.rem(row, 2)
    half = col // 2
    slot = lax.rem(col, 2)
    rows = basis_v.shape[0]
    cols = basis_v.shape[1]
    piece = cols // (2 * PLANES)
    per_col = cols // PANEL
    carried = rows // 2
    unit = carried // UNITS
    portion = carried // PARTS

    def at(r, c):
        return (grp, r, c)

    def along(step):
        return at(lax.rem(plane + PLANES + step, PLANES) * 2 + core, col)

    twin = at(row + 1 - 2 * core, col)
    above = along(1)
    below = along(-1)
    pair = at(row, col + 1 - 2 * slot)
    mirror = at(row, 3 - col)
    across = at(row, lax.rem(col + 2, COLS))

    load_basis = pltpu.make_async_copy(basis_hbm, basis_v, load_sem.at[0])
    load_matrix = pltpu.make_async_copy(matrix_hbm, matrix_v, load_sem.at[1])
    load_basis.start()

    barrier = pltpu.get_barrier_semaphore()
    partners = (twin, above, below, along(2), along(-2), pair, mirror, across)
    for other in partners:
        pl.semaphore_signal(barrier, inc=1, device_id=other, device_id_type=MESH)

    sends = []

    def send(src, dst, send_sem, recv_sem, target):
        copy = pltpu.make_async_remote_copy(
            src_ref=src, dst_ref=dst, send_sem=send_sem, recv_sem=recv_sem,
            device_id=target, device_id_type=MESH,
        )
        copy.start()
        sends.append(copy)

    def arrived(ref, sem):
        pltpu.make_async_copy(ref, ref, sem).wait()

    load_basis.wait()
    load_matrix.start()
    span_rows = min(64, carried)

    def pick(s, i, row_half):
        index = index_ref[half, s] - slot * per_col
        at_rows = pl.ds(pl.multiple_of(row_half * carried + i * span_rows, span_rows), span_rows)
        index_v = jnp.full((span_rows, PANEL), index, jnp.int32)
        total = jnp.zeros((span_rows, PANEL), F32)
        for j in range(per_col):
            total = jnp.where(index_v == j, basis_v[at_rows, j * PANEL:(j + 1) * PANEL], total)
        return total

    def pick_other(i, carry):
        for s in range(PASSES):
            at_rows = pl.ds(pl.multiple_of(i * span_rows, span_rows), span_rows)
            pair_out[s, at_rows] = pick(s, i, 1 - slot)
        return carry

    def pick_own(i, carry):
        for s in range(PASSES):
            at_rows = pl.ds(pl.multiple_of(i * span_rows, span_rows), span_rows)
            ring[0, s, at_rows] = pick(s, i, slot)
        return carry

    lax.fori_loop(0, carried // span_rows, pick_other, 0)
    pl.semaphore_wait(barrier, len(partners))

    def of_unit(u):
        return pl.ds(u * unit, unit)

    def of_portion(v):
        return pl.ds(v * portion, portion)

    for s in range(PASSES):
        for u in range(UNITS):
            send(
                pair_out.at[s, of_unit(u)], pair_in.at[s, of_unit(u)],
                pair_s.at[s, u], pair_r.at[s, u], pair,
            )
    lax.fori_loop(0, carried // span_rows, pick_own, 0)

    def split_matrix(b):
        at_cols = pl.ds(b * 2 * PANEL, 2 * PANEL)
        m_high[:, at_cols], m_low[:, at_cols] = split(matrix_v[:, at_cols])

    def split_basis(b):
        at_cols = pl.ds(b * 2 * PANEL, 2 * PANEL)
        q_high[:, at_cols], q_low[:, at_cols] = split(basis_v[:, at_cols])

    matrix_work = [functools.partial(split_matrix, b) for b in range(cols // (2 * PANEL))]
    basis_work = [functools.partial(split_basis, b) for b in range(cols // (2 * PANEL))]

    def do(work, count):
        for _ in range(min(count, len(work))):
            work.pop(0)()

    cross = []

    def deliver(s, d, v):
        source = lax.rem(plane + PLANES - d, PLANES)
        target = source // 2
        odd = lax.rem(source, 2)
        src = ring.at[d, s, of_portion(v)]
        first = pl.multiple_of(slot * carried + v * portion, portion)
        dst = chosen.at[2 * odd + core, 2 * half + s, pl.ds(first, portion)]
        sem = cross_r.at[odd, s, col, v]
        copy = pltpu.make_async_remote_copy(
            src_ref=src, dst_ref=dst, send_sem=cross_s.at[d, s, v], recv_sem=sem,
            device_id=at(row, target), device_id_type=MESH,
        )

        @pl.when(target != col)
        def _():
            copy.start()

        @pl.when(target == col)
        def _():
            pltpu.make_async_copy(src, dst, sem).start()

        cross.append((target, copy))

    def go_up(s, d, u):
        send(
            ring.at[d, s, of_unit(u)], ring.at[d + 1, s, of_unit(u)],
            up_s.at[d, s, u], up_r.at[d, s, u], above,
        )

    def go_down(s, d, u):
        send(
            ring.at[(PLANES - d) % PLANES, s, of_unit(u)],
            ring.at[PLANES - 1 - d, s, of_unit(u)],
            down_s.at[d, s, u], down_r.at[d, s, u], below,
        )

    def handle(s, d):
        for u in range(UNITS):
            up_far, down_far = u % 2 == 0, u % 2 == 1
            if d == 0:
                arrived(pair_in.at[s, of_unit(u)], pair_r.at[s, u])
                ring[0, s, of_unit(u)] = ring[0, s, of_unit(u)] + pair_in[s, of_unit(u)]
                go_up(s, 0, u)
                go_down(s, 0, u)
            if d > 0 and (d < 4 or up_far):
                arrived(ring.at[d, s, of_unit(u)], up_r.at[d - 1, s, u])
                if d < 3 or (d == 3 and up_far):
                    go_up(s, d, u)
            if d > 0 and (d < 4 or down_far):
                arrived(ring.at[PLANES - d, s, of_unit(u)], down_r.at[d - 1, s, u])
                if d < 3 or (d == 3 and down_far):
                    go_down(s, d, u)
            if u % 2 == 1:
                deliver(s, d, u // 2)
                if 0 < d < 4:
                    deliver(s, PLANES - d, u // 2)

    def share(s, odd):
        for v in range(PARTS):
            for c in range(COLS):
                first = (c % 2) * carried + v * portion
                ref = chosen.at[2 * odd + core, 2 * (c // 2) + s, pl.ds(first, portion)]
                arrived(ref, cross_r.at[odd, s, c, v])
                send(ref, ref, twin_s.at[odd, s, c, v], twin_r.at[odd, s, c, v], twin)

    def shared(s, odd):
        for v in range(PARTS):
            for c in range(COLS):
                first = (c % 2) * carried + v * portion
                ref = chosen.at[2 * odd + 1 - core, 2 * (c // 2) + s, pl.ds(first, portion)]
                arrived(ref, twin_r.at[odd, s, c, v])

    def multiply(s, block, first, rest=None):
        value = jnp.concatenate([chosen[block, s], chosen[block, 2 + s]], axis=1)
        x_high[...], x_low[...] = split(value)
        at_cols = pl.ds(pl.multiple_of(block * rows, rows), rows)

        def body(i, carry):
            at_rows = pl.ds(i * carried if rest else pl.multiple_of(i * carried, carried), carried)
            term = dot3(m_high[at_rows, at_cols], m_low[at_rows, at_cols], x_high[...], x_low[...])
            for h in range(2):
                piece_h = term[:, h * PANEL:(h + 1) * PANEL]
                image[s, h, at_rows] = piece_h if first else image[s, h, at_rows] + piece_h
            return carry
        if rest is None:
            lax.fori_loop(0, 2, body, 0)
        else:
            for i in range(2):
                body(i, 0)
                for v in range(i * SWAPS // 2, (i + 1) * SWAPS // 2):
                    rest(s, v)

    def half_rows(v):
        return pl.ds(v * (rows // SWAPS), rows // SWAPS)

    def swap(s, v):
        send(
            image.at[s, 1 - half, half_rows(v)], image_in.at[s, half_rows(v)],
            swap_s.at[s, v], swap_r.at[s, v], mirror,
        )

    def add_swap(s, v):
        at_rows = half_rows(v)
        arrived(image_in.at[s, at_rows], swap_r.at[s, v])
        image_sum[s, at_rows] = image[s, half, at_rows] + image_in[s, at_rows]
        send(
            image_sum.at[s, at_rows], image_pair.at[s, at_rows],
            half_s.at[s, v], half_r.at[s, v], pair,
        )

    order = (4, 3, 5, 2, 6, 1, 7, 0)
    groups = ((0, 3), (3, 8))

    def project(s, parity, group):
        for i in range(*groups[group]):
            target = lax.rem(plane + order[i], PLANES)
            at_cols = pl.ds(pl.multiple_of((2 * target + parity) * piece, piece), piece)
            proj[s, parity, i] = dot3(
                y_high[s], y_low[s], q_high[:, at_cols], q_low[:, at_cols]
            )

    def begin(s):
        for v in range(SWAPS):
            arrived(image_pair.at[s, half_rows(v)], half_r.at[s, v])
        y_high[s], y_low[s] = split((image_sum[s] + image_pair[s]).T)

    def exchange(s, group):
        first, last = groups[group]
        span_i = pl.ds(first, last - first)
        project(s, 1 - core, group)
        send(
            proj.at[s, 1 - core, span_i], proj_in.at[s, span_i],
            mate_s.at[s, group], mate_r.at[s, group], twin,
        )
        project(s, core, group)

    def combine(s, group):
        first, last = groups[group]
        span_i = pl.ds(first, last - first)
        arrived(proj_in.at[s, span_i], mate_r.at[s, group])
        proj_sum[s, span_i] = proj[s, core, span_i] + proj_in[s, span_i]

    near_rows = piece // 2

    def whole(sign):
        return pl.ds(0, near_rows) if sign == 0 else pl.ds(near_rows, near_rows)

    def place(sign, d):
        return order.index(d if sign == 0 else PLANES - d)

    def toward(sign, d):
        return along(d if sign == 0 else -d)

    def sum_far(s):
        for sign in range(2):
            send(
                proj_sum.at[s, place(sign, 4), whole(sign)], far_in.at[s, sign, 1, whole(sign)],
                far_s.at[s, sign, 1], far_r.at[s, sign, 1], toward(sign, 2),
            )
            send(
                proj_sum.at[s, place(sign, 3)], far_in.at[s, sign, 0],
                far_s.at[s, sign, 0], far_r.at[s, sign, 0], toward(sign, 1),
            )

    def sum_near(s):
        for sign in range(2):
            send(
                proj_sum.at[s, place(sign, 1)], near_in.at[s, sign],
                near_s.at[s, sign], near_r.at[s, sign], toward(sign, 1),
            )

    def sum_mid(s):
        for sign in range(2):
            arrived(far_in.at[s, sign, 1, whole(sign)], far_r.at[s, sign, 1])
            arrived(far_in.at[s, sign, 0], far_r.at[s, sign, 0])
            mid_out[s, sign] = proj_sum[s, place(sign, 2)] + far_in[s, sign, 0]
            mid_out[s, sign, whole(sign)] = mid_out[s, sign, whole(sign)] + far_in[s, sign, 1, whole(sign)]
            send(
                mid_out.at[s, sign], mid_in.at[s, sign],
                mid_s.at[s, sign], mid_r.at[s, sign], toward(sign, 2),
            )

    def finish(s):
        total = proj_sum[s, order.index(0)]
        for sign in range(2):
            arrived(near_in.at[s, sign], near_r.at[s, sign])
            arrived(mid_in.at[s, sign], mid_r.at[s, sign])
            total = total + near_in[s, sign] + mid_in[s, sign]
        out_ref[:, s * PANEL:(s + 1) * PANEL] = total.T

    handle(0, 0)
    load_matrix.wait()
    do(matrix_work, 2)
    handle(0, 1)
    do(matrix_work, 2)
    handle(0, 2)
    do(matrix_work, 2)
    handle(1, 0)
    do(matrix_work, 2)
    handle(0, 3)
    do(basis_work, 0)
    handle(1, 1)
    do(basis_work, 0)
    handle(0, 4)
    do(basis_work, 0)
    handle(1, 2)
    do(basis_work, 0)
    handle(1, 3)
    do(basis_work, 0)
    handle(1, 4)
    do(basis_work, 0)
    share(0, 0)
    share(0, 1)
    multiply(0, core, True)
    multiply(0, 2 + core, False)
    shared(0, 0)
    multiply(0, 1 - core, False)
    shared(0, 1)
    multiply(0, 3 - core, False, swap)
    share(1, 0)
    share(1, 1)
    multiply(1, core, True)
    multiply(1, 2 + core, False)
    add_swap(0, 0)
    add_swap(0, 1)
    add_swap(0, 2)
    add_swap(0, 3)
    shared(1, 0)
    multiply(1, 1 - core, False)
    shared(1, 1)
    multiply(1, 3 - core, False, swap)
    do(basis_work, 16)
    begin(0)
    exchange(0, 0)
    combine(0, 0)
    sum_far(0)
    add_swap(1, 0)
    add_swap(1, 1)
    exchange(0, 1)
    add_swap(1, 2)
    add_swap(1, 3)
    combine(0, 1)
    sum_near(0)
    sum_mid(0)
    begin(1)
    exchange(1, 0)
    combine(1, 0)
    sum_far(1)
    exchange(1, 1)
    combine(1, 1)
    sum_near(1)
    sum_mid(1)
    finish(0)
    finish(1)
    for copy in sends:
        copy.wait_send()
    for target, copy in cross:
        @pl.when(target != col)
        def _(copy=copy):
            copy.wait_send()


def body(matrix, basis_matrix, panel_index):
    rows, cols = matrix.shape
    piece = cols // (2 * PLANES)
    carried = rows // 2
    vmem = pltpu.VMEM

    def pairs(*shape):
        return [pltpu.SemaphoreType.DMA(shape), pltpu.SemaphoreType.DMA(shape)]

    return pl.pallas_call(
        kernel,
        out_shape=jax.ShapeDtypeStruct((piece, 2 * PANEL), F32),
        in_specs=[
            pl.BlockSpec(memory_space=pltpu.SMEM),
            pl.BlockSpec(memory_space=pl.ANY),
            pl.BlockSpec(memory_space=pl.ANY),
        ],
        out_specs=pl.BlockSpec(memory_space=pltpu.VMEM),
        scratch_shapes=[
            vmem((rows, cols), F32),
            vmem((rows, cols), F32),
            vmem((rows, cols), BF16),
            vmem((rows, cols), BF16),
            vmem((rows, cols), BF16),
            vmem((rows, cols), BF16),
            vmem((PASSES, carried, PANEL), F32),
            vmem((PASSES, carried, PANEL), F32),
            vmem((PLANES, PASSES, carried, PANEL), F32),
            vmem((4, COLS, rows, PANEL), F32),
            vmem((rows, 2 * PANEL), BF16),
            vmem((rows, 2 * PANEL), BF16),
            vmem((PASSES, PANEL, rows), BF16),
            vmem((PASSES, PANEL, rows), BF16),
            vmem((PASSES, 2, rows, PANEL), F32),
            vmem((PASSES, rows, PANEL), F32),
            vmem((PASSES, rows, PANEL), F32),
            vmem((PASSES, rows, PANEL), F32),
            vmem((PASSES, 2, PLANES, piece, PANEL), F32),
            vmem((PASSES, PLANES, piece, PANEL), F32),
            vmem((PASSES, PLANES, piece, PANEL), F32),
            vmem((PASSES, 2, 2, piece, PANEL), F32),
            vmem((PASSES, 2, piece, PANEL), F32),
            vmem((PASSES, 2, piece, PANEL), F32),
            vmem((PASSES, 2, piece, PANEL), F32),
            pltpu.SemaphoreType.DMA((2,)),
            *pairs(PASSES, UNITS),
            *pairs(4, PASSES, UNITS),
            *pairs(4, PASSES, UNITS),
            pltpu.SemaphoreType.DMA((PLANES, PASSES, PARTS)),
            pltpu.SemaphoreType.DMA((2, PASSES, COLS, PARTS)),
            *pairs(2, PASSES, COLS, PARTS),
            *pairs(PASSES, SWAPS),
            *pairs(PASSES, SWAPS),
            *pairs(PASSES, 2),
            *pairs(PASSES, 2, 2),
            *pairs(PASSES, 2),
            *pairs(PASSES, 2),
        ],
        compiler_params=pltpu.CompilerParams(
            collective_id=0, has_side_effects=True, vmem_limit_bytes=56 * 2**20
        ),
        name="project_panels",
    )(panel_index, matrix, basis_matrix)


def solution(mesh):
    return jax.shard_map(
        body,
        mesh=mesh,
        in_specs=(P(("grp", "row"), "col"), P(("grp", "row"), "col"), P("grp", None)),
        out_specs=P(("grp", "col", "row"), None),
        check_vma=False,
    )
```
